128 devices in a mesh: blk: 8 (over z, y_lo), group: 16 (over y_hi, x, core).
Axes of the slice: x: 4, y: 4 (y_hi: 2, y_lo: 2; y = y_hi * 2 + y_lo), z: 4, core: 2. Of those that a mesh axis runs over, the one named last changes fastest.
Arguments:
- image_embeds: float32 [32768, 1152], P(('blk', 'group')), may hold values from -8.5 to 8.5
- text_embeds: float32 [32768, 1152], P(('blk', 'group')), may hold values from -8.5 to 8.5
- log_scale: float32 [1], replicated, may hold values from 4 to 4.8
- bias: float32 [1], replicated, may hold values from -6 to -3
Outputs:
- loss: float32 [1], replicated
- grad_image: float32 [32768, 1152], P(('blk', 'group'))
- grad_text: float32 [32768, 1152], P(('blk', 'group'))
- grad_log_scale: float32 [1], replicated
- grad_bias: float32 [1], replicated
The draws below stay inside these ranges and needn't reach their ends.
All inputs are finite; a program needn't handle non-finite values.
Results may differ from the reference program's by a relative error of at most 0.00045.
Values may be sent and summed in bfloat16 or wider, within the bound.
No kernel may reach another device: no remote copies, remote signals or barrier semaphores. Data moves between devices by JAX's collectives and lax.ppermute only.
A program may use at most 192 MiB of HBM per device.

```python
import jax
import jax.numpy as jnp
from jax import lax

D = 1152
STEPS = 2
ROWS = 32768
N_BLK = 8


def shared_line(key):
    return jnp.clip(jax.random.normal(key, (D,), jnp.float32), -6.0, 6.0)


def build_rows(noise, line, lead, slope):
    place = jnp.arange(ROWS, dtype=jnp.float32)[:, None] / ROWS
    return noise + (lead + slope * place) * line[None, :]


def draw_image_embeds(key, part):
    line = shared_line(key)
    key = jax.random.fold_in(key, 11)
    noise = jnp.clip(jax.random.normal(key, (ROWS, D), jnp.float32), -6.0, 6.0)
    return build_rows(noise, line, 0.05, 0.3)


def draw_text_embeds(key, part):
    line = shared_line(key)
    key = jax.random.fold_in(key, 23)
    noise = jnp.clip(jax.random.normal(key, (ROWS, D), jnp.float32), -6.0, 6.0)
    return build_rows(noise, line, 0.05, 0.3)


def setup_inputs(seed: int = 0) -> dict:
    keys = jax.random.split(jax.random.key(seed), 5)
    image_embeds = draw_image_embeds(jax.random.fold_in(keys[4], 71), 0)
    text_embeds = draw_text_embeds(jax.random.fold_in(keys[4], 71), 0)
    log_scale = jnp.clip(jax.random.uniform(keys[2], (1,), jnp.float32, 4.0, 4.8), 4.0, 4.8)
    bias = jnp.clip(jax.random.uniform(keys[3], (1,), jnp.float32, -6.0, -3.0), -6.0, -3.0)
    return dict(image_embeds=image_embeds, text_embeds=text_embeds, log_scale=log_scale, bias=bias)


eps = 1e-06

def unit_rows(embeds):
    length = jnp.sqrt(lax.optimization_barrier(jnp.sum(embeds * embeds, axis=1, keepdims=True)) + eps)
    return (embeds / length, length)

def reference(image_embeds, text_embeds, log_scale, bias):
    block_size = ROWS // N_BLK
    image_unit, image_length = unit_rows(image_embeds)
    text_unit, text_length = unit_rows(text_embeds)
    image_half = image_unit.astype(jnp.bfloat16)
    text_half = text_unit.astype(jnp.bfloat16)
    scale_value = jnp.exp(log_scale[0])
    bias_value = bias[0]
    diagonal = jnp.eye(block_size, dtype=jnp.bool_)
    image_acc = jnp.zeros((ROWS, D), jnp.float32)
    text_acc = jnp.zeros((ROWS, D), jnp.float32)
    loss_sum = jnp.float32(0.0)
    weight_sum = jnp.float32(0.0)
    dot_sum = jnp.float32(0.0)
    for block_num in range(N_BLK):
        image_block = image_half[block_num * block_size:(block_num + 1) * block_size]
        block_acc = jnp.zeros((block_size, D), jnp.float32)
        for section_num in range(STEPS):
            other = (block_num - section_num) % N_BLK
            text_block = text_half[other * block_size:(other + 1) * block_size]
            dots = jnp.dot(image_block, text_block.T, preferred_element_type=jnp.float32)
            logits = scale_value * dots + bias_value
            if section_num == 0:
                signs = jnp.where(diagonal, jnp.float32(1.0), jnp.float32(-1.0))
            else:
                signs = jnp.full(dots.shape, -1.0, jnp.float32)
            loss_sum = loss_sum + jnp.sum(jax.nn.softplus(-signs * logits))
            weights = -signs * jax.nn.sigmoid(-signs * logits)
            weight_sum = weight_sum + jnp.sum(weights)
            dot_sum = dot_sum + jnp.sum(weights * dots)
            weights_half = weights.astype(jnp.bfloat16)
            block_acc = block_acc + jnp.dot(weights_half, text_block, preferred_element_type=jnp.float32)
            text_acc = text_acc.at[other * block_size:(other + 1) * block_size].add(jnp.dot(weights_half.T, image_block, preferred_element_type=jnp.float32))
        image_acc = image_acc.at[block_num * block_size:(block_num + 1) * block_size].set(block_acc)
    grad_image = scale_value * (image_acc - image_unit * lax.optimization_barrier(jnp.sum(image_unit * image_acc, axis=1, keepdims=True))) / image_length
    grad_text = scale_value * (text_acc - text_unit * lax.optimization_barrier(jnp.sum(text_unit * text_acc, axis=1, keepdims=True))) / text_length
    loss = (loss_sum / ROWS).reshape(1)
    grad_log_scale = (scale_value * dot_sum / ROWS).reshape(1)
    grad_bias = (weight_sum / ROWS).reshape(1)
    return (loss, grad_image, grad_text, grad_log_scale, grad_bias)
```

```python
import jax
import jax.numpy as jnp
from jax import lax
from jax.experimental import pallas as pl
from jax.experimental.pallas import tpu as pltpu
from jax.sharding import PartitionSpec as P

AXES = ("blk", "group")
EPS = 1e-06
LOG2E = 1.4426950408889634
LN2 = 0.6931471805599453
ROWS = 256
CHUNK = 16
LANES = 256
VMEM_LIMIT = 60 * 1024 * 1024


def place_index(z, y, x, core):
    z, y, x, core = z % 4, y % 4, x % 4, core % 2
    return (z * 2 + y % 2) * 16 + (y // 2) * 8 + x * 2 + core


def places():
    return [(z, y, x, c) for z in range(4) for y in range(4) for x in range(4) for c in range(2)]


def send(value, moved, back=False):
    pairs = [(place_index(*place), place_index(*moved(*place))) for place in places()]
    if back:
        pairs = [(target, source) for source, target in pairs]
    return lax.ppermute(value, AXES, pairs)


def other_core(z, y, x, c):
    return z, y, x, 1 - c


def x_up(z, y, x, c):
    return z, y, x + 1, c


def x_down(z, y, x, c):
    return z, y, x - 1, c


def x_far(z, y, x, c):
    return z, y, x + 2, c


def y_far(z, y, x, c):
    return z, y + 2, x, c


def before_up(z, y, x, c):
    return (z, y + 1, x, c) if y % 2 else (z - 1, y + 1, x, c)


def before_down(z, y, x, c):
    return (z, y - 1, x, c) if y % 2 else (z - 1, y - 1, x, c)


def z_up(z, y, x, c):
    return z + 1, y, x, c


def z_down(z, y, x, c):
    return z - 1, y, x, c


def z_far(z, y, x, c):
    return z + 2, y, x, c


TEXT_MOVES = (x_up, x_down, x_far)
IMAGE_MOVES = (y_far, before_up, before_down)
Z_MOVES = (z_up, z_down, z_far)


def halves_kernel(image_ref, text_ref, image_half_ref, text_half_ref):
    for ref, half_ref in ((image_ref, image_half_ref), (text_ref, text_half_ref)):
        rows = ref[...]
        length = jnp.sqrt(jnp.sum(rows * rows, axis=1, keepdims=True) + EPS)
        half_ref[...] = (rows / length).astype(jnp.bfloat16)


def halves(image_embeds, text_embeds):
    shape = jax.ShapeDtypeStruct(image_embeds.shape, jnp.bfloat16)
    return pl.pallas_call(
        halves_kernel,
        out_shape=(shape, shape),
        compiler_params=pltpu.CompilerParams(vmem_limit_bytes=VMEM_LIMIT),
        name="halves",
    )(image_embeds, text_embeds)


def log1p(value):
    small = value * (1.0 - value * (0.5 - value * (1.0 / 3.0)))
    return jnp.where(value < 1e-3, small, jnp.log(1.0 + value))


def fold_lanes(value):
    total = value[:, 0:128]
    for first in range(128, value.shape[1], 128):
        total = total + value[:, first : first + 128]
    return total


def pair_terms(dots_ref, weights_ref, first_row, rows, first_col, cols, scale, shift, sums_ref, marked):
    def body(step, carry):
        relu, weight_sum, dot_sum, product = carry
        start = pl.multiple_of(first_row + step * CHUNK, CHUNK)
        dots = dots_ref[pl.ds(start, CHUNK), first_col : first_col + cols]
        logits = dots * scale + shift
        decay = jnp.exp2(jnp.minimum(logits, -logits))
        above = 1.0 + decay
        share = pl.reciprocal(above, approx=True)
        share = share * (2.0 - above * share)
        if marked:
            row = lax.broadcasted_iota(jnp.int32, (CHUNK, cols), 0) + step * CHUNK
            same = row == lax.broadcasted_iota(jnp.int32, (CHUNK, cols), 1)
            logits = jnp.where(same, -logits, logits)
        weights = jnp.where(logits >= 0, share, decay * share)
        if marked:
            weights = jnp.where(same, -weights, weights)
        weights_ref[pl.ds(start, CHUNK), first_col : first_col + cols] = weights.astype(jnp.bfloat16)
        positive = jnp.maximum(logits, 0.0)
        weighted = weights * dots
        for first in range(0, CHUNK, 8):
            part = slice(first, first + 8)
            relu = relu + positive[part]
            weight_sum = weight_sum + weights[part]
            dot_sum = dot_sum + weighted[part]
            product = product * above[part] + decay[part]
        return relu, weight_sum, dot_sum, product

    zero = jnp.zeros((8, cols), jnp.float32)
    relu, weight_sum, dot_sum, product = lax.fori_loop(
        0, rows // CHUNK, body, (zero, zero, zero, zero), unroll=4
    )
    sums_ref[0] += fold_lanes(relu) * LN2 + fold_lanes(log1p(product))
    sums_ref[1] += fold_lanes(weight_sum)
    sums_ref[2] += fold_lanes(dot_sum)


def largest(value):
    return fold_max(jnp.max(jnp.abs(value).reshape(value.shape[0] // 8, 8, value.shape[1]), axis=0))


def fold_max(value):
    total = value[:, 0:128]
    for first in range(128, value.shape[1], 128):
        total = jnp.maximum(total, value[:, first : first + 128])
    return total


def pairs_kernel(
    scalars_ref, text_ref, mine_ref, other_ref,
    text_acc_ref, mine_acc_ref, other_acc_ref, sums_ref,
    dots_ref, weights_ref,
):
    step = pl.program_id(0)
    scale, shift = scalars_ref[0], scalars_ref[1]
    texts = text_ref.shape[0]

    @pl.when(step == 0)
    def _():
        sums_ref[...] = jnp.zeros_like(sums_ref)

    for place, ref in enumerate((mine_ref, other_ref)):
        dots_ref[place * ROWS : (place + 1) * ROWS, :] = lax.dot_general(
            ref[...], text_ref[...], (((1,), (1,)), ((), ())), preferred_element_type=jnp.float32
        )

    @pl.when(step == 0)
    def _():
        pair_terms(dots_ref, weights_ref, 0, ROWS, 0, LANES, scale, shift, sums_ref, True)

    @pl.when(step != 0)
    def _():
        pair_terms(dots_ref, weights_ref, 0, ROWS, 0, LANES, scale, shift, sums_ref, False)

    for first in range(LANES, texts, LANES):
        pair_terms(dots_ref, weights_ref, 0, ROWS, first, LANES, scale, shift, sums_ref, False)
    for first in range(0, texts, LANES):
        pair_terms(dots_ref, weights_ref, ROWS, ROWS, first, LANES, scale, shift, sums_ref, False)

    back = jnp.zeros((texts, text_ref.shape[1]), jnp.float32)
    for place, (ref, acc_ref) in enumerate(((mine_ref, mine_acc_ref), (other_ref, other_acc_ref))):
        weights = weights_ref[place * ROWS : (place + 1) * ROWS, :]
        acc = jnp.dot(weights, text_ref[...], preferred_element_type=jnp.float32)
        acc_ref[...] = acc
        sums_ref[3] = jnp.maximum(sums_ref[3], largest(acc))
        back = back + lax.dot_general(
            weights, ref[...], (((0,), (0,)), ((), ())), preferred_element_type=jnp.float32
        )

    @pl.when(step == 0)
    def _():
        text_acc_ref[...] = back

    @pl.when(step != 0)
    def _():
        text_acc_ref[...] += back

    @pl.when(step == pl.num_programs(0) - 1)
    def _():
        sums_ref[4] = largest(text_acc_ref[...])


def pairs(scalars, texts, mine, other):
    count, width = texts.shape
    steps = mine.shape[0] // ROWS
    rows = pl.BlockSpec((ROWS, width), lambda k: (k, 0))
    whole = pl.BlockSpec((count, width), lambda k: (0, 0))
    return pl.pallas_call(
        pairs_kernel,
        grid=(steps,),
        in_specs=[pl.BlockSpec(memory_space=pltpu.SMEM), whole, rows, rows],
        out_specs=[whole, rows, rows, pl.BlockSpec((5, 8, 128), lambda k: (0, 0, 0))],
        out_shape=[
            jax.ShapeDtypeStruct((count, width), jnp.float32),
            jax.ShapeDtypeStruct(mine.shape, jnp.float32),
            jax.ShapeDtypeStruct(other.shape, jnp.float32),
            jax.ShapeDtypeStruct((5, 8, 128), jnp.float32),
        ],
        scratch_shapes=[
            pltpu.VMEM((2 * ROWS, count), jnp.float32),
            pltpu.VMEM((2 * ROWS, count), jnp.bfloat16),
        ],
        compiler_params=pltpu.CompilerParams(vmem_limit_bytes=VMEM_LIMIT),
        cost_estimate=pl.CostEstimate(
            flops=6 * count * 2 * mine.shape[0] * width, bytes_accessed=20_000_000, transcendentals=4_000_000
        ),
        name="pairs",
    )(scalars, texts, mine, other)


def tangent_part(scale_value, embeds, accum):
    length = jnp.sqrt(jnp.sum(embeds * embeds, axis=1, keepdims=True) + EPS)
    unit = embeds / length
    return scale_value * (accum - unit * jnp.sum(unit * accum, axis=1, keepdims=True)) / length


def factor_of(limit):
    return 1024.0 / jnp.maximum(limit, 1e-35)


def packed(value, factor):
    return (value * factor).astype(jnp.float16)


def on_device(image_embeds, text_embeds, log_scale, bias):
    image_half, text_half = halves(image_embeds, text_embeds)
    scale_value = jnp.exp(log_scale[0])
    scalars = jnp.stack([scale_value * LOG2E, bias[0] * LOG2E])
    texts = jnp.concatenate([text_half] + [send(text_half, move) for move in TEXT_MOVES], axis=0)
    mine = jnp.concatenate([image_half] + [send(image_half, move) for move in IMAGE_MOVES], axis=0)
    other = send(mine, other_core)
    text_acc, mine_acc, other_acc, sums = pairs(scalars, texts, mine, other)

    folded = jnp.concatenate([jnp.sum(sums[:3], axis=(1, 2)), jnp.max(sums[3:], axis=(1, 2))])
    neighbour = send(jnp.broadcast_to(folded[:, None], (5, 128)), other_core)[:, 0]
    totals = folded[:3] + neighbour[:3]
    image_factor = factor_of(folded[3] + neighbour[3])
    text_factor = factor_of(folded[4])

    text_back = []
    small = jnp.broadcast_to(jnp.concatenate([totals, 1.0 / text_factor[None]])[:, None], (4, 128))
    for place, move in enumerate(TEXT_MOVES):
        rows = text_acc[(place + 1) * ROWS : (place + 2) * ROWS]
        text_back.append((send(packed(rows, text_factor), move, back=True), send(small, move, back=True)[:, 0]))

    mine_acc = mine_acc + send(other_acc, other_core)
    totals = (totals + text_back[2][1][:3]) + (text_back[0][1][:3] + text_back[1][1][:3])
    image_back = []
    small = jnp.broadcast_to(jnp.concatenate([totals, 1.0 / image_factor[None]])[:, None], (4, 128))
    for place, move in enumerate(IMAGE_MOVES):
        rows = mine_acc[(place + 1) * ROWS : (place + 2) * ROWS]
        image_back.append((send(packed(rows, image_factor), move, back=True), send(small, move, back=True)[:, 0]))
    own_parity = totals + image_back[0][1][:3]
    other_parity = image_back[1][1][:3] + image_back[2][1][:3]
    odd = lax.axis_index("blk") % 2 == 1
    totals = jnp.concatenate(
        [jnp.where(odd, other_parity, own_parity), jnp.where(odd, own_parity, other_parity)]
    )
    small = jnp.broadcast_to(totals[:, None], (6, 128))
    from_up, from_down, from_far = (send(small, move)[:, 0] for move in Z_MOVES)
    totals = (totals + from_far) + (from_up + from_down)
    totals = totals[:3] + totals[3:]

    text_sum, image_sum = text_acc[:ROWS], mine_acc[:ROWS]
    for rows, numbers in text_back:
        text_sum = text_sum + rows.astype(jnp.float32) * numbers[3]
    for rows, numbers in image_back:
        image_sum = image_sum + rows.astype(jnp.float32) * numbers[3]
    grad_text = tangent_part(scale_value, text_embeds, text_sum)
    grad_image = tangent_part(scale_value, image_embeds, image_sum)
    total_rows = ROWS * lax.axis_size("blk") * lax.axis_size("group")
    loss = (totals[0] / total_rows).reshape(1)
    grad_bias = (totals[1] / total_rows).reshape(1)
    grad_log_scale = (scale_value * totals[2] / total_rows).reshape(1)
    return (loss, grad_image, grad_text, grad_log_scale, grad_bias)


def solution(mesh):
    return jax.shard_map(
        on_device,
        mesh=mesh,
        in_specs=(P(AXES, None), P(AXES, None), P(), P()),
        out_specs=(P(), P(AXES, None), P(AXES, None), P(), P()),
        check_vma=False,
    )
```

```python
import functools

import jax
import jax.numpy as jnp
from jax import lax
from jax.experimental import pallas as pl
from jax.experimental.pallas import tpu as pltpu
from jax.sharding import PartitionSpec as P

AXES = ("blk", "group")
EPS = 1e-06
LOG2E = 1.4426950408889634
LN2 = 0.6931471805599453
ROWS = 256
BLOCK = 272
CHUNK = 16
LANES = 128
VMEM_LIMIT = 44 * 1024 * 1024


def place_index(z, y, x, core):
    z, y, x, core = z % 4, y % 4, x % 4, core % 2
    return (z * 2 + y % 2) * 16 + (y // 2) * 8 + x * 2 + core


def places():
    return [(z, y, x, c) for z in range(4) for y in range(4) for x in range(4) for c in range(2)]


def send(value, moved, back=False):
    pairs = [(place_index(*place), place_index(*moved(*place))) for place in places()]
    if back:
        pairs = [(target, source) for source, target in pairs]
    return lax.ppermute(value, AXES, pairs)


def other_core(z, y, x, c):
    return z, y, x, 1 - c


def x_up(z, y, x, c):
    return z, y, x + 1, c


def x_down(z, y, x, c):
    return z, y, x - 1, c


def x_far(z, y, x, c):
    return z, y, x + 2, c


def y_far(z, y, x, c):
    return z, y + 2, x, c


def before_up(z, y, x, c):
    return (z, y + 1, x, c) if y % 2 else (z - 1, y + 1, x, c)


def before_down(z, y, x, c):
    return (z, y - 1, x, c) if y % 2 else (z - 1, y - 1, x, c)


TEXT_MOVES = (x_up, x_down, x_far)
IMAGE_MOVES = (y_far, before_up, before_down)
FAR_MOVES = (
    lambda z, y, x, c: (z, y ^ 1, x, c),
    lambda z, y, x, c: (z, y ^ 2, x, c),
    lambda z, y, x, c: (z ^ 1, y, x, c),
    lambda z, y, x, c: (z ^ 2, y, x, c),
)
NEAR_MOVES = (
    lambda z, y, x, c: (z, y, x ^ 1, c),
    lambda z, y, x, c: (z, y, x ^ 2, c),
    other_core,
)


def halves_kernel(image_ref, text_ref, image_half_ref, text_half_ref):
    for ref, half_ref in ((image_ref, image_half_ref), (text_ref, text_half_ref)):
        rows = ref[...]
        length = jnp.sqrt(jnp.sum(rows * rows, axis=1, keepdims=True) + EPS)
        half_ref[...] = (rows / length).astype(jnp.bfloat16)


def halves(image_embeds, text_embeds):
    shape = jax.ShapeDtypeStruct(image_embeds.shape, jnp.bfloat16)
    return pl.pallas_call(
        halves_kernel,
        out_shape=(shape, shape),
        name="halves",
    )(image_embeds, text_embeds)


def log1p(value):
    small = value * (1.0 - value * (0.5 - value * (1.0 / 3.0)))
    return jnp.where(value < 1e-3, small, jnp.log(1.0 + value))


def pair_terms(dots_ref, weights_ref, scale, shift, sums_ref, first_step):
    rows, cols = dots_ref.shape
    offset = jnp.where(first_step, 0, -2 * rows)
    for first_col in range(0, cols, LANES):
        relu = weight_sum = dot_sum = product = jnp.zeros((8, LANES), jnp.float32)
        for first_row in range(0, rows, CHUNK):
            place = (slice(first_row, first_row + CHUNK), slice(first_col, first_col + LANES))
            dots = dots_ref[place]
            logits = dots * scale + shift
            decay = jnp.exp2(jnp.minimum(logits, -logits))
            above = 1.0 + decay
            share = pl.reciprocal(above, approx=True)
            share = share * (2.0 - above * share)
            marked = first_row < ROWS and first_col <= first_row < first_col + LANES
            if marked:
                row = lax.broadcasted_iota(jnp.int32, (CHUNK, LANES), 0) + first_row
                col = lax.broadcasted_iota(jnp.int32, (CHUNK, LANES), 1) + first_col
                same = row - col == offset
                logits = jnp.where(same, -logits, logits)
            weights = jnp.where(logits >= 0, share, decay * share)
            if marked:
                weights = jnp.where(same, -weights, weights)
            weights_ref[place] = weights.astype(jnp.bfloat16)
            positive = jnp.maximum(logits, 0.0)
            weighted = weights * dots
            for first in range(0, CHUNK, 8):
                part = slice(first, first + 8)
                relu = relu + positive[part]
                weight_sum = weight_sum + weights[part]
                dot_sum = dot_sum + weighted[part]
                product = product * above[part] + decay[part]
        sums_ref[0] += relu * LN2 + log1p(product)
        sums_ref[1] += weight_sum
        sums_ref[2] += dot_sum


def largest(value):
    return fold_max(jnp.max(jnp.abs(value).reshape(value.shape[0] // 8, 8, value.shape[1]), axis=0))


def fold_max(value):
    total = value[:, 0:128]
    for first in range(128, value.shape[1], 128):
        total = jnp.maximum(total, value[:, first : first + 128])
    return total


def power_of(limit):
    return jnp.floor(jnp.log2(jnp.maximum(limit, 1e-30))) + 1.0


def pairs_kernel(count, earlier, last, *refs):
    refs = list(refs)
    take = lambda number: [refs.pop(0) for _ in range(number)]
    (scalars_ref,) = take(1)
    text_refs, mine_refs, other_refs = take(4), take(count), take(count)
    prior_text_ref, prior_sums_ref = take(2) if earlier else (None, None)
    mine_acc_ref, other_acc_ref = take(2)
    back_refs = take(4) if last else None
    text_acc_ref, sums_ref = take(2)
    text_ref, images_ref, dots_ref, weights_ref, limit_ref = refs
    step = pl.program_id(0)
    scale, shift = scalars_ref[0], scalars_ref[1]
    width = text_ref.shape[1]

    @pl.when(step == 0)
    def _():
        sums_ref[...] = prior_sums_ref[...] if earlier else jnp.zeros_like(sums_ref)
        limit_ref[...] = jnp.zeros_like(limit_ref)
        for place, ref in enumerate(text_refs):
            text_ref[place * ROWS : (place + 1) * ROWS, :] = ref[...]

    for place in range(count):

        @pl.when(step == place)
        def _():
            images_ref[:ROWS, :] = mine_refs[place][...]
            images_ref[ROWS:, :] = other_refs[place][...]

    dots_ref[...] = lax.dot_general(
        images_ref[...], text_ref[...], (((1,), (1,)), ((), ())), preferred_element_type=jnp.float32
    )
    pair_terms(dots_ref, weights_ref, scale, shift, sums_ref, step == 0 if not earlier else step < 0)
    acc = jnp.dot(weights_ref[...], text_ref[...], preferred_element_type=jnp.float32)
    limit_ref[...] = jnp.maximum(limit_ref[...], largest(acc))
    mine_acc_ref[:ROWS, :] = acc[:ROWS]
    other_acc_ref[:ROWS, :] = acc[ROWS:]
    row = lax.broadcasted_iota(jnp.int32, (8, width), 0)
    sums = jnp.zeros((8, width), jnp.float32)
    for place in range(3):
        sums = jnp.where(row == place, jnp.sum(sums_ref[place]), sums)
    power = power_of(jnp.full((8, width), jnp.max(limit_ref[...])))
    for ref in (mine_acc_ref, other_acc_ref):
        ref[ROWS : ROWS + 8, :] = sums
        ref[ROWS + 8 :, :] = power
    back = lax.dot_general(
        weights_ref[...], images_ref[...], (((0,), (0,)), ((), ())), preferred_element_type=jnp.float32
    )
    if earlier:
        text_acc_ref[...] = prior_text_ref[...] + back
    else:

        @pl.when(step == 0)
        def _():
            text_acc_ref[...] = back

        @pl.when(step != 0)
        def _():
            text_acc_ref[...] += back

    if last:
        back_refs[0][...] = text_acc_ref[:ROWS, :]
        power = power_of(jnp.full((8, width), jnp.max(largest(text_acc_ref[ROWS:, :])))) - 10.0
        factor = jnp.exp2(-power)[:1]
        for place, ref in enumerate(back_refs[1:]):
            ref[:ROWS, :] = text_acc_ref[(place + 1) * ROWS : (place + 2) * ROWS, :] * factor
            ref[ROWS:, :] = jnp.concatenate([power, power], axis=0)


def pairs(scalars, texts, mine, other, prior=None):
    width = mine[0].shape[1]
    count = len(mine)
    last = prior is not None
    rows = 4 * ROWS
    unit = pl.BlockSpec((ROWS, width), lambda k: (0, 0))
    block = pl.BlockSpec((BLOCK, width), lambda k: (0, 0))
    each = pl.BlockSpec((BLOCK, width), lambda k: (k, 0))
    whole = pl.BlockSpec((rows, width), lambda k: (0, 0))
    sums = pl.BlockSpec((3, 8, 128), lambda k: (0, 0, 0))

    def shape(*dims):
        return jax.ShapeDtypeStruct(dims, jnp.float32)

    in_specs = [pl.BlockSpec(memory_space=pltpu.SMEM)] + [unit] * (4 + 2 * count)
    operands = [scalars, *texts, *mine, *other]
    out_specs = [each, each]
    out_shape = [shape(count * BLOCK, width)] * 2
    scratch = []
    if last:
        in_specs += [whole, sums]
        operands += prior
        out_specs += [unit, block, block, block]
        out_shape += [shape(ROWS, width)] + [shape(BLOCK, width)] * 3
        scratch += [pltpu.VMEM((rows, width), jnp.float32), pltpu.VMEM((3, 8, 128), jnp.float32)]
    else:
        out_specs += [whole, sums]
        out_shape += [shape(rows, width), shape(3, 8, 128)]
    return pl.pallas_call(
        functools.partial(pairs_kernel, count, last, last),
        grid=(count,),
        in_specs=in_specs,
        out_specs=out_specs,
        out_shape=out_shape,
        scratch_shapes=scratch
        + [
            pltpu.VMEM((rows, width), jnp.bfloat16),
            pltpu.VMEM((2 * ROWS, width), jnp.bfloat16),
            pltpu.VMEM((2 * ROWS, rows), jnp.float32),
            pltpu.VMEM((2 * ROWS, rows), jnp.bfloat16),
            pltpu.VMEM((8, 128), jnp.float32),
        ],
        compiler_params=pltpu.CompilerParams(vmem_limit_bytes=VMEM_LIMIT),
        cost_estimate=pl.CostEstimate(
            flops=(20 if last else 6) * rows * 2 * count * ROWS * width, bytes_accessed=1 << 20, transcendentals=3 * rows * 2 * count * ROWS
        ),
        name="pairs",
    )(*operands)


def tangent_kernel(scalars_ref, embeds_ref, accum_ref, out_ref):
    embeds = embeds_ref[...]
    accum = accum_ref[...]
    length = jnp.sqrt(jnp.sum(embeds * embeds, axis=1, keepdims=True) + EPS)
    inverse = 1.0 / length
    unit = embeds * inverse
    along = jnp.sum(unit * accum, axis=1, keepdims=True)
    out_ref[...] = (accum - unit * along) * (scalars_ref[2] * inverse)


def tangent_part(scalars, embeds, accum):
    return pl.pallas_call(
        tangent_kernel,
        in_specs=[pl.BlockSpec(memory_space=pltpu.SMEM)] + [pl.BlockSpec(memory_space=pltpu.VMEM)] * 2,
        out_shape=jax.ShapeDtypeStruct(embeds.shape, jnp.float32),
        name="tangent",
    )(scalars, embeds, accum)


def groups(rows):
    return rows.reshape(rows.shape[0] // 8, 8, rows.shape[1])


def packed(mine, other):
    mine, other = groups(mine), groups(other)
    power = jnp.maximum(mine[-1:], other[-1:]) - 9.0
    group = lax.broadcasted_iota(jnp.int32, mine.shape, 0)
    rows = jnp.where(group < ROWS // 8, (mine + other) * jnp.exp2(-power), power)
    return rows.astype(jnp.float16).reshape(BLOCK, -1)


def unpacked(rows):
    rows = groups(rows).astype(jnp.float32)
    return (rows[: ROWS // 8] * jnp.exp2(rows[-1:])).reshape(ROWS, -1)


def after(value, *others):
    return lax.optimization_barrier((value, *others))[0]


def on_device(image_embeds, text_embeds, log_scale, bias):
    image_half, text_half = halves(image_embeds, text_embeds)
    scale_value = jnp.exp(log_scale[0])
    scalars = jnp.stack([scale_value * LOG2E, bias[0] * LOG2E, scale_value])
    above = send(image_half, before_up)
    below = send(image_half, before_down)
    texts = [text_half] + [send(text_half, move) for move in TEXT_MOVES]
    beside = send(image_half, other_core)
    opposite = send(image_half, y_far)
    first = [image_half, above, below]
    first_other = [beside, send(above, other_core), send(below, other_core)]
    second_other = send(opposite, other_core)

    mine, other, text_acc, sums = pairs(scalars, texts, first, first_other)
    from_core = send(other, other_core)
    second, other, back0, back1, back2, back3 = pairs(
        scalars, texts, [opposite], [second_other], [text_acc, sums]
    )
    second_from_core = send(other, other_core)

    blocks = [slice(place * BLOCK, (place + 1) * BLOCK) for place in range(3)]
    packs = [
        packed(second, second_from_core),
        packed(mine[blocks[1]], from_core[blocks[1]]),
        packed(mine[blocks[2]], from_core[blocks[2]]),
    ]
    totals, *packs = lax.optimization_barrier((second[ROWS : ROWS + 8, :128], *packs))
    opposite, above, below = [send(rows, move, back=True) for rows, move in zip(packs, IMAGE_MOVES)]
    for move in NEAR_MOVES:
        totals = totals + send(totals, move)
    back1, back2, back3 = after((back1, back2, back3), totals)
    up = send(back1.astype(jnp.float16), x_up, back=True)
    down = send(back2.astype(jnp.float16), x_down, back=True)
    far = send(back3.astype(jnp.float16), x_far, back=True)
    totals = after(totals, above, below, opposite)
    for move in FAR_MOVES:
        totals = totals + send(totals, move)
    totals = totals[:3, 0] / (ROWS * lax.axis_size("blk") * lax.axis_size("group"))

    text_sum = back0
    for rows in (up, down, far):
        text_sum = text_sum + unpacked(rows)
    image_sum = mine[:ROWS] + from_core[:ROWS]
    for rows in (opposite, above, below):
        image_sum = image_sum + unpacked(rows)
    grad_text = tangent_part(scalars, text_embeds, text_sum)
    grad_image = tangent_part(scalars, image_embeds, image_sum)
    return (totals[0:1], grad_image, grad_text, scale_value * totals[2:3], totals[1:2])


def solution(mesh):
    return jax.shard_map(
        on_device,
        mesh=mesh,
        in_specs=(P(AXES, None), P(AXES, None), P(), P()),
        out_specs=(P(), P(AXES, None), P(AXES, None), P(), P()),
        check_vma=False,
    )
```

```python
import functools

import jax
import jax.numpy as jnp
from jax import lax
from jax.experimental import pallas as pl
from jax.experimental.pallas import tpu as pltpu
from jax.sharding import PartitionSpec as P

AXES = ("blk", "group")
EPS = 1e-06
LOG2E = 1.4426950408889634
LN2 = 0.6931471805599453
ROWS = 256
BLOCK = 272
CHUNK = 16
LANES = 128
VMEM_LIMIT = 44 * 1024 * 1024


def place_index(z, y, x, core):
    z, y, x, core = z % 4, y % 4, x % 4, core % 2
    return (z * 2 + y % 2) * 16 + (y // 2) * 8 + x * 2 + core


def places():
    return [(z, y, x, c) for z in range(4) for y in range(4) for x in range(4) for c in range(2)]


def send(value, moved, back=False):
    pairs = [(place_index(*place), place_index(*moved(*place))) for place in places()]
    if back:
        pairs = [(target, source) for source, target in pairs]
    return lax.ppermute(value, AXES, pairs)


def other_core(z, y, x, c):
    return z, y, x, 1 - c


def x_up(z, y, x, c):
    return z, y, x + 1, c


def x_down(z, y, x, c):
    return z, y, x - 1, c


def x_far(z, y, x, c):
    return z, y, x + 2, c


def y_far(z, y, x, c):
    return z, y + 2, x, c


def before_up(z, y, x, c):
    return (z, y + 1, x, c) if y % 2 else (z - 1, y + 1, x, c)


def before_down(z, y, x, c):
    return (z, y - 1, x, c) if y % 2 else (z - 1, y - 1, x, c)


TEXT_MOVES = (x_up, x_down, x_far)
IMAGE_MOVES = (y_far, before_up, before_down)
NEAR_MOVES = (
    lambda z, y, x, c: (z, y, x ^ 1, c),
    lambda z, y, x, c: (z, y, x ^ 2, c),
    other_core,
)
FAR_MOVES = (
    lambda z, y, x, c: (z ^ 1, y, x, c),
    lambda z, y, x, c: (z ^ 2, y, x, c),
    lambda z, y, x, c: (z, y ^ 1, x, c),
    lambda z, y, x, c: (z, y ^ 2, x, c),
)


def halves_kernel(image_ref, text_ref, image_half_ref, text_half_ref):
    for ref, half_ref in ((image_ref, image_half_ref), (text_ref, text_half_ref)):
        rows = ref[...]
        length = jnp.sqrt(jnp.sum(rows * rows, axis=1, keepdims=True) + EPS)
        half_ref[...] = (rows / length).astype(jnp.bfloat16)


def halves(image_embeds, text_embeds):
    shape = jax.ShapeDtypeStruct(image_embeds.shape, jnp.bfloat16)
    return pl.pallas_call(
        halves_kernel,
        out_shape=(shape, shape),
        name="halves",
    )(image_embeds, text_embeds)


def log1p(value):
    small = value * (1.0 - value * (0.5 - value * (1.0 / 3.0)))
    return jnp.where(value < 1e-3, small, jnp.log(1.0 + value))


def pair_terms(dots_ref, weights_ref, scale, shift, sums_ref, first_step):
    rows, cols = dots_ref.shape
    offset = jnp.where(first_step, 0, -2 * rows)
    for first_col in range(0, cols, LANES):
        relu = weight_sum = dot_sum = product = jnp.zeros((8, LANES), jnp.float32)
        for first_row in range(0, rows, CHUNK):
            place = (slice(first_row, first_row + CHUNK), slice(first_col, first_col + LANES))
            dots = dots_ref[place]
            logits = dots * scale + shift
            decay = jnp.exp2(jnp.minimum(logits, -logits))
            above = 1.0 + decay
            share = pl.reciprocal(above, approx=True)
            share = share * (2.0 - above * share)
            marked = first_row < ROWS and first_col <= first_row < first_col + LANES
            if marked:
                row = lax.broadcasted_iota(jnp.int32, (CHUNK, LANES), 0) + first_row
                col = lax.broadcasted_iota(jnp.int32, (CHUNK, LANES), 1) + first_col
                same = row - col == offset
                logits = jnp.where(same, -logits, logits)
            weights = jnp.where(logits >= 0, share, decay * share)
            if marked:
                weights = jnp.where(same, -weights, weights)
            weights_ref[place] = weights.astype(jnp.bfloat16)
            positive = jnp.maximum(logits, 0.0)
            weighted = weights * dots
            for first in range(0, CHUNK, 8):
                part = slice(first, first + 8)
                relu = relu + positive[part]
                weight_sum = weight_sum + weights[part]
                dot_sum = dot_sum + weighted[part]
                product = product * above[part] + decay[part]
        sums_ref[0] += relu * LN2 + log1p(product)
        sums_ref[1] += weight_sum
        sums_ref[2] += dot_sum


def largest(value):
    return fold_max(jnp.max(jnp.abs(value).reshape(value.shape[0] // 8, 8, value.shape[1]), axis=0))


def fold_max(value):
    total = value[:, 0:128]
    for first in range(128, value.shape[1], 128):
        total = jnp.maximum(total, value[:, first : first + 128])
    return total


def power_of(limit):
    return jnp.floor(jnp.log2(jnp.maximum(limit, 1e-30))) + 1.0


def pairs_kernel(count, earlier, last, *refs):
    refs = list(refs)
    take = lambda number: [refs.pop(0) for _ in range(number)]
    (scalars_ref,) = take(1)
    text_refs, mine_refs, other_refs = take(4), take(count), take(count)
    prior_text_ref, prior_sums_ref = take(2) if earlier else (None, None)
    mine_acc_ref, other_acc_ref = take(2)
    back_refs = take(4) if last else None
    text_acc_ref, sums_ref = take(2)
    text_ref, images_ref, dots_ref, weights_ref, limit_ref = refs
    step = pl.program_id(0)
    scale, shift = scalars_ref[0], scalars_ref[1]
    width = text_ref.shape[1]

    @pl.when(step == 0)
    def _():
        sums_ref[...] = prior_sums_ref[...] if earlier else jnp.zeros_like(sums_ref)
        limit_ref[...] = jnp.zeros_like(limit_ref)
        for place, ref in enumerate(text_refs):
            text_ref[place * ROWS : (place + 1) * ROWS, :] = ref[...]

    for place in range(count):

        @pl.when(step == place)
        def _():
            images_ref[:ROWS, :] = mine_refs[place][...]
            images_ref[ROWS:, :] = other_refs[place][...]

    dots_ref[...] = lax.dot_general(
        images_ref[...], text_ref[...], (((1,), (1,)), ((), ())), preferred_element_type=jnp.float32
    )
    pair_terms(dots_ref, weights_ref, scale, shift, sums_ref, step == 0 if not earlier else step < 0)
    acc = jnp.dot(weights_ref[...], text_ref[...], preferred_element_type=jnp.float32)
    limit_ref[...] = jnp.maximum(limit_ref[...], largest(acc))
    mine_acc_ref[:ROWS, :] = acc[:ROWS]
    other_acc_ref[:ROWS, :] = acc[ROWS:]
    row = lax.broadcasted_iota(jnp.int32, (8, width), 0)
    sums = jnp.zeros((8, width), jnp.float32)
    for place in range(3):
        sums = jnp.where(row == place, jnp.sum(sums_ref[place]), sums)
    power = power_of(jnp.full((8, width), jnp.max(limit_ref[...])))
    for ref in (mine_acc_ref, other_acc_ref):
        ref[ROWS : ROWS + 8, :] = sums
        ref[ROWS + 8 :, :] = power
    back = lax.dot_general(
        weights_ref[...], images_ref[...], (((0,), (0,)), ((), ())), preferred_element_type=jnp.float32
    )
    if earlier:
        text_acc_ref[...] = prior_text_ref[...] + back
    else:

        @pl.when(step == 0)
        def _():
            text_acc_ref[...] = back

        @pl.when(step != 0)
        def _():
            text_acc_ref[...] += back

    if last:
        back_refs[0][...] = text_acc_ref[:ROWS, :]
        power = power_of(jnp.full((8, width), jnp.max(largest(text_acc_ref[ROWS:, :])))) - 10.0
        factor = jnp.exp2(-power)[:1]
        for place, ref in enumerate(back_refs[1:]):
            ref[:ROWS, :] = text_acc_ref[(place + 1) * ROWS : (place + 2) * ROWS, :] * factor
            ref[ROWS:, :] = jnp.concatenate([power, power], axis=0)


def pairs(scalars, texts, mine, other, prior=None):
    width = mine[0].shape[1]
    count = len(mine)
    last = prior is not None
    rows = 4 * ROWS
    unit = pl.BlockSpec((ROWS, width), lambda k: (0, 0))
    block = pl.BlockSpec((BLOCK, width), lambda k: (0, 0))
    each = pl.BlockSpec((BLOCK, width), lambda k: (k, 0))
    whole = pl.BlockSpec((rows, width), lambda k: (0, 0))
    sums = pl.BlockSpec((3, 8, 128), lambda k: (0, 0, 0))

    def shape(*dims):
        return jax.ShapeDtypeStruct(dims, jnp.float32)

    in_specs = [pl.BlockSpec(memory_space=pltpu.SMEM)] + [unit] * (4 + 2 * count)
    operands = [scalars, *texts, *mine, *other]
    out_specs = [each, each]
    out_shape = [shape(count * BLOCK, width)] * 2
    scratch = []
    if last:
        in_specs += [whole, sums]
        operands += prior
        out_specs += [unit, block, block, block]
        out_shape += [shape(ROWS, width)] + [shape(BLOCK, width)] * 3
        scratch += [pltpu.VMEM((rows, width), jnp.float32), pltpu.VMEM((3, 8, 128), jnp.float32)]
    else:
        out_specs += [whole, sums]
        out_shape += [shape(rows, width), shape(3, 8, 128)]
    return pl.pallas_call(
        functools.partial(pairs_kernel, count, last, last),
        grid=(count,),
        in_specs=in_specs,
        out_specs=out_specs,
        out_shape=out_shape,
        scratch_shapes=scratch
        + [
            pltpu.VMEM((rows, width), jnp.bfloat16),
            pltpu.VMEM((2 * ROWS, width), jnp.bfloat16),
            pltpu.VMEM((2 * ROWS, rows), jnp.float32),
            pltpu.VMEM((2 * ROWS, rows), jnp.bfloat16),
            pltpu.VMEM((8, 128), jnp.float32),
        ],
        compiler_params=pltpu.CompilerParams(vmem_limit_bytes=VMEM_LIMIT),
        cost_estimate=pl.CostEstimate(
            flops=(20 if last else 6) * rows * 2 * count * ROWS * width, bytes_accessed=1 << 20, transcendentals=3 * rows * 2 * count * ROWS
        ),
        name="pairs",
    )(*operands)


def tangent_kernel(scalars_ref, embeds_ref, accum_ref, out_ref):
    embeds = embeds_ref[...]
    accum = accum_ref[...]
    length = jnp.sqrt(jnp.sum(embeds * embeds, axis=1, keepdims=True) + EPS)
    inverse = 1.0 / length
    unit = embeds * inverse
    along = jnp.sum(unit * accum, axis=1, keepdims=True)
    out_ref[...] = (accum - unit * along) * (scalars_ref[2] * inverse)


def tangent_part(scalars, embeds, accum):
    return pl.pallas_call(
        tangent_kernel,
        in_specs=[pl.BlockSpec(memory_space=pltpu.SMEM)] + [pl.BlockSpec(memory_space=pltpu.VMEM)] * 2,
        out_shape=jax.ShapeDtypeStruct(embeds.shape, jnp.float32),
        name="tangent",
    )(scalars, embeds, accum)


def groups(rows):
    return rows.reshape(rows.shape[0] // 8, 8, rows.shape[1])


def packed(mine, other):
    mine, other = groups(mine), groups(other)
    power = jnp.maximum(mine[-1:], other[-1:]) - 9.0
    group = lax.broadcasted_iota(jnp.int32, mine.shape, 0)
    rows = jnp.where(group < ROWS // 8, (mine + other) * jnp.exp2(-power), power)
    return rows.astype(jnp.float16).reshape(BLOCK, -1)


def unpacked(rows):
    rows = groups(rows).astype(jnp.float32)
    return (rows[: ROWS // 8] * jnp.exp2(rows[-1:])).reshape(ROWS, -1)


def after(value, *others):
    return lax.optimization_barrier((value, *others))[0]


def on_device(image_embeds, text_embeds, log_scale, bias):
    image_half, text_half = halves(image_embeds, text_embeds)
    scale_value = jnp.exp(log_scale[0])
    scalars = jnp.stack([scale_value * LOG2E, bias[0] * LOG2E, scale_value])
    above = send(image_half, before_up)
    below = send(image_half, before_down)
    texts = [text_half] + [send(text_half, move) for move in TEXT_MOVES]
    beside = send(image_half, other_core)
    opposite = send(after(image_half, above), y_far)
    first = [image_half, above, below]
    first_other = [beside, send(above, other_core), send(below, other_core)]

    mine, other, text_acc, sums = pairs(scalars, texts, first, first_other)
    second_other = send(after(opposite, sums), other_core)
    from_core = send(after(other, second_other), other_core)
    second, other, back0, back1, back2, back3 = pairs(
        scalars, texts, [opposite], [second_other], [text_acc, sums]
    )
    second_from_core = send(other, other_core)

    blocks = [slice(place * BLOCK, (place + 1) * BLOCK) for place in range(3)]
    above = packed(mine[blocks[1]], from_core[blocks[1]])
    below = packed(mine[blocks[2]], from_core[blocks[2]])
    totals, above, below, second_from_core = lax.optimization_barrier(
        (second[ROWS : ROWS + 8, :128], above, below, second_from_core)
    )
    opposite = packed(second, second_from_core)
    above = send(above, before_up, back=True)
    below = send(below, before_down, back=True)
    for move in NEAR_MOVES:
        totals = totals + send(totals, move)
    back1, back2, back3, opposite = after((back1, back2, back3, opposite), totals)
    up = send(back1.astype(jnp.float16), x_up, back=True)
    down = send(back2.astype(jnp.float16), x_down, back=True)
    far = send(after(back3, up, down).astype(jnp.float16), x_far, back=True)
    opposite = send(opposite, y_far, back=True)
    totals = after(totals, above, below, opposite)
    for move in FAR_MOVES:
        totals = totals + send(totals, move)
    totals = totals[:3, 0] / (ROWS * lax.axis_size("blk") * lax.axis_size("group"))

    text_sum = back0
    for rows in (up, down, far):
        text_sum = text_sum + unpacked(rows)
    image_sum = mine[:ROWS] + from_core[:ROWS]
    for rows in (opposite, above, below):
        image_sum = image_sum + unpacked(rows)
    grad_text = tangent_part(scalars, text_embeds, text_sum)
    grad_image = tangent_part(scalars, image_embeds, image_sum)
    return (totals[0:1], grad_image, grad_text, scale_value * totals[2:3], totals[1:2])


def solution(mesh):
    return jax.shard_map(
        on_device,
        mesh=mesh,
        in_specs=(P(AXES, None), P(AXES, None), P(), P()),
        out_specs=(P(), P(AXES, None), P(AXES, None), P(), P()),
        check_vma=False,
    )
```

```python
import functools

import jax
import jax.numpy as jnp
from jax import lax
from jax.experimental import pallas as pl
from jax.experimental.pallas import tpu as pltpu
from jax.sharding import PartitionSpec as P

AXES = ("blk", "group")
EPS = 1e-06
LOG2E = 1.4426950408889634
LN2 = 0.6931471805599453
ROWS = 256
BLOCK = 272
CHUNK = 16
LANES = 128
VMEM_LIMIT = 32 * 1024 * 1024


def place_index(z, y, x, core):
    z, y, x, core = z % 4, y % 4, x % 4, core % 2
    return (z * 2 + y % 2) * 16 + (y // 2) * 8 + x * 2 + core


def places():
    return [(z, y, x, c) for z in range(4) for y in range(4) for x in range(4) for c in range(2)]


def send(value, moved, back=False):
    pairs = [(place_index(*place), place_index(*moved(*place))) for place in places()]
    if back:
        pairs = [(target, source) for source, target in pairs]
    return lax.ppermute(value, AXES, pairs)


def other_core(z, y, x, c):
    return z, y, x, 1 - c


def x_up(z, y, x, c):
    return z, y, x + 1, c


def x_down(z, y, x, c):
    return z, y, x - 1, c


def x_far(z, y, x, c):
    return z, y, x + 2, c


def y_far(z, y, x, c):
    return z, y + 2, x, c


def before_up(z, y, x, c):
    return (z, y + 1, x, c) if y % 2 else (z - 1, y + 1, x, c)


def before_down(z, y, x, c):
    return (z, y - 1, x, c) if y % 2 else (z - 1, y - 1, x, c)


TEXT_MOVES = (x_up, x_down, x_far)
IMAGE_MOVES = (y_far, before_up, before_down)
NEAR_MOVES = (
    lambda z, y, x, c: (z, y, x ^ 1, c),
    lambda z, y, x, c: (z, y, x ^ 2, c),
    other_core,
)
FAR_MOVES = (
    lambda z, y, x, c: (z ^ 1, y, x, c),
    lambda z, y, x, c: (z ^ 2, y, x, c),
    lambda z, y, x, c: (z, y ^ 1, x, c),
    lambda z, y, x, c: (z, y ^ 2, x, c),
)


PARTS = 4


def part_copies(sources, targets, sems):
    rows = ROWS // PARTS
    return [
        [
            pltpu.make_async_copy(
                source.at[pl.ds(part * rows, rows)], target.at[pl.ds(part * rows, rows)], sems.at[part, place]
            )
            for place, (source, target) in enumerate(zip(sources, targets))
        ]
        for part in range(PARTS)
    ]


def by_parts(work, sources, held, results, targets, in_sems, out_sems):
    inward = part_copies(sources, held, in_sems)
    outward = part_copies(results, targets, out_sems)
    for copies in inward:
        for copy in copies:
            copy.start()
    for part in range(PARTS):
        for copy in inward[part]:
            copy.wait()
        work(slice(part * (ROWS // PARTS), (part + 1) * (ROWS // PARTS)))
        for copy in outward[part]:
            copy.start()
    for copies in outward:
        for copy in copies:
            copy.wait()


def halves_kernel(image_ref, text_ref, image_half_ref, text_half_ref, *buffers):
    held, results, sems = buffers[:2], buffers[2:4], buffers[4:]

    def work(part):
        for ref, half_ref in zip(held, results):
            rows = ref[part, :]
            length = jnp.sqrt(jnp.sum(rows * rows, axis=1, keepdims=True) + EPS)
            half_ref[part, :] = (rows * (1.0 / length)).astype(jnp.bfloat16)

    by_parts(work, (image_ref, text_ref), held, results, (image_half_ref, text_half_ref), *sems)


def halves(image_embeds, text_embeds):
    shape = image_embeds.shape
    half = jax.ShapeDtypeStruct(shape, jnp.bfloat16)
    anywhere = pl.BlockSpec(memory_space=pl.ANY)
    return pl.pallas_call(
        halves_kernel,
        in_specs=[anywhere] * 2,
        out_specs=[anywhere] * 2,
        out_shape=(half, half),
        scratch_shapes=[pltpu.VMEM(shape, jnp.float32)] * 2
        + [pltpu.VMEM(shape, jnp.bfloat16)] * 2
        + [pltpu.SemaphoreType.DMA((PARTS, 2))] * 2,
        name="halves",
    )(image_embeds, text_embeds)


def log1p(value):
    small = value * (1.0 - value * (0.5 - value * (1.0 / 3.0)))
    return jnp.where(value < 1e-3, small, jnp.log(1.0 + value))


def pair_terms(dots_ref, weights_ref, scale, shift, sums_ref, first_step):
    rows, cols = dots_ref.shape
    offset = jnp.where(first_step, 0, -2 * rows)
    for first_col in range(0, cols, LANES):
        relu = weight_sum = dot_sum = product = jnp.zeros((8, LANES), jnp.float32)
        for first_row in range(0, rows, CHUNK):
            place = (slice(first_row, first_row + CHUNK), slice(first_col, first_col + LANES))
            dots = dots_ref[place]
            logits = dots * scale + shift
            decay = jnp.exp2(jnp.minimum(logits, -logits))
            above = 1.0 + decay
            share = pl.reciprocal(above, approx=True)
            share = share * (2.0 - above * share)
            marked = first_row < ROWS and first_col <= first_row < first_col + LANES
            if marked:
                row = lax.broadcasted_iota(jnp.int32, (CHUNK, LANES), 0) + first_row
                col = lax.broadcasted_iota(jnp.int32, (CHUNK, LANES), 1) + first_col
                same = row - col == offset
                logits = jnp.where(same, -logits, logits)
            weights = jnp.where(logits >= 0, share, decay * share)
            if marked:
                weights = jnp.where(same, -weights, weights)
            weights_ref[place] = weights.astype(jnp.bfloat16)
            positive = jnp.maximum(logits, 0.0)
            weighted = weights * dots
            for first in range(0, CHUNK, 8):
                part = slice(first, first + 8)
                relu = relu + positive[part]
                weight_sum = weight_sum + weights[part]
                dot_sum = dot_sum + weighted[part]
                product = product * above[part] + decay[part]
        sums_ref[0] += relu * LN2 + log1p(product)
        sums_ref[1] += weight_sum
        sums_ref[2] += dot_sum


def largest(value):
    return fold_max(jnp.max(jnp.abs(value).reshape(value.shape[0] // 8, 8, value.shape[1]), axis=0))


def fold_max(value):
    total = value[:, 0:128]
    for first in range(128, value.shape[1], 128):
        total = jnp.maximum(total, value[:, first : first + 128])
    return total


def power_of(limit):
    return jnp.floor(jnp.log2(jnp.maximum(limit, 1e-30))) + 1.0


def pairs_kernel(count, earlier, last, *refs):
    refs = list(refs)
    take = lambda number: [refs.pop(0) for _ in range(number)]
    (scalars_ref,) = take(1)
    text_refs, mine_refs, other_refs = take(4), take(count), take(count)
    prior_text_ref, prior_sums_ref = take(2) if earlier else (None, None)
    mine_acc_ref, other_acc_ref = take(2)
    back_refs = take(4) if last else None
    text_acc_ref, sums_ref = take(2)
    text_ref, images_ref, dots_ref, weights_ref, limit_ref = refs
    step = pl.program_id(0)
    scale, shift = scalars_ref[0], scalars_ref[1]
    width = text_ref.shape[1]

    @pl.when(step == 0)
    def _():
        sums_ref[...] = prior_sums_ref[...] if earlier else jnp.zeros_like(sums_ref)
        limit_ref[...] = jnp.zeros_like(limit_ref)
        for place, ref in enumerate(text_refs):
            text_ref[place * ROWS : (place + 1) * ROWS, :] = ref[...]

    for place in range(count):

        @pl.when(step == place)
        def _():
            images_ref[:ROWS, :] = mine_refs[place][...]
            images_ref[ROWS:, :] = other_refs[place][...]

    dots_ref[...] = lax.dot_general(
        images_ref[...], text_ref[...], (((1,), (1,)), ((), ())), preferred_element_type=jnp.float32
    )
    pair_terms(dots_ref, weights_ref, scale, shift, sums_ref, step == 0 if not earlier else step < 0)
    acc = jnp.dot(weights_ref[...], text_ref[...], preferred_element_type=jnp.float32)
    limit_ref[...] = jnp.maximum(limit_ref[...], largest(acc))
    mine_acc_ref[:ROWS, :] = acc[:ROWS]
    other_acc_ref[:ROWS, :] = acc[ROWS:]
    row = lax.broadcasted_iota(jnp.int32, (8, width), 0)
    sums = jnp.zeros((8, width), jnp.float32)
    for place in range(3):
        sums = jnp.where(row == place, jnp.sum(sums_ref[place]), sums)
    power = power_of(jnp.full((8, width), jnp.max(limit_ref[...])))
    for ref in (mine_acc_ref, other_acc_ref):
        ref[ROWS : ROWS + 8, :] = sums
        ref[ROWS + 8 :, :] = power
    back = lax.dot_general(
        weights_ref[...], images_ref[...], (((0,), (0,)), ((), ())), preferred_element_type=jnp.float32
    )
    if earlier:
        text_acc_ref[...] = prior_text_ref[...] + back
    else:

        @pl.when(step == 0)
        def _():
            text_acc_ref[...] = back

        @pl.when(step != 0)
        def _():
            text_acc_ref[...] += back

    if last:
        back_refs[0][...] = text_acc_ref[:ROWS, :]
        power = power_of(jnp.full((8, width), jnp.max(largest(text_acc_ref[ROWS:, :])))) - 10.0
        factor = jnp.exp2(-power)[:1]
        for place, ref in enumerate(back_refs[1:]):
            ref[:ROWS, :] = text_acc_ref[(place + 1) * ROWS : (place + 2) * ROWS, :] * factor
            ref[ROWS:, :] = jnp.concatenate([power, power], axis=0)


def pairs(scalars, texts, mine, other, prior=None):
    width = mine[0].shape[1]
    count = len(mine)
    last = prior is not None
    rows = 4 * ROWS
    unit = pl.BlockSpec((ROWS, width), lambda k: (0, 0))
    block = pl.BlockSpec((BLOCK, width), lambda k: (0, 0))
    each = pl.BlockSpec((BLOCK, width), lambda k: (k, 0))
    whole = pl.BlockSpec((rows, width), lambda k: (0, 0))
    sums = pl.BlockSpec((3, 8, 128), lambda k: (0, 0, 0))

    def shape(*dims):
        return jax.ShapeDtypeStruct(dims, jnp.float32)

    in_specs = [pl.BlockSpec(memory_space=pltpu.SMEM)] + [unit] * (4 + 2 * count)
    operands = [scalars, *texts, *mine, *other]
    out_specs = [each, each]
    out_shape = [shape(count * BLOCK, width)] * 2
    scratch = []
    if last:
        in_specs += [whole, sums]
        operands += prior
        out_specs += [unit, block, block, block]
        out_shape += [shape(ROWS, width)] + [shape(BLOCK, width)] * 3
        scratch += [pltpu.VMEM((rows, width), jnp.float32), pltpu.VMEM((3, 8, 128), jnp.float32)]
    else:
        out_specs += [whole, sums]
        out_shape += [shape(rows, width), shape(3, 8, 128)]
    return pl.pallas_call(
        functools.partial(pairs_kernel, count, last, last),
        grid=(count,),
        in_specs=in_specs,
        out_specs=out_specs,
        out_shape=out_shape,
        scratch_shapes=scratch
        + [
            pltpu.VMEM((rows, width), jnp.bfloat16),
            pltpu.VMEM((2 * ROWS, width), jnp.bfloat16),
            pltpu.VMEM((2 * ROWS, rows), jnp.float32),
            pltpu.VMEM((2 * ROWS, rows), jnp.bfloat16),
            pltpu.VMEM((8, 128), jnp.float32),
        ],
        compiler_params=pltpu.CompilerParams(vmem_limit_bytes=VMEM_LIMIT),
        cost_estimate=pl.CostEstimate(
            flops=(20 if last else 6) * rows * 2 * count * ROWS * width, bytes_accessed=1 << 20, transcendentals=3 * rows * 2 * count * ROWS
        ),
        name="pairs",
    )(*operands)


def tangent_kernel(scalars_ref, embeds_ref, accum_ref, out_ref):
    embeds = embeds_ref[...]
    accum = accum_ref[...]
    length = jnp.sqrt(jnp.sum(embeds * embeds, axis=1, keepdims=True) + EPS)
    inverse = 1.0 / length
    unit = embeds * inverse
    along = jnp.sum(unit * accum, axis=1, keepdims=True)
    out_ref[...] = (accum - unit * along) * (scalars_ref[2] * inverse)


def tangent_part(scalars, embeds, accum):
    return pl.pallas_call(
        tangent_kernel,
        in_specs=[pl.BlockSpec(memory_space=pltpu.SMEM)] + [pl.BlockSpec(memory_space=pltpu.VMEM)] * 2,
        out_shape=jax.ShapeDtypeStruct(embeds.shape, jnp.float32),
        name="tangent",
    )(scalars, embeds, accum)


def groups(rows):
    return rows.reshape(rows.shape[0] // 8, 8, rows.shape[1])


def packed(mine, other):
    mine, other = groups(mine), groups(other)
    power = jnp.maximum(mine[-1:], other[-1:]) - 9.0
    group = lax.broadcasted_iota(jnp.int32, mine.shape, 0)
    rows = jnp.where(group < ROWS // 8, (mine + other) * jnp.exp2(-power), power)
    return rows.astype(jnp.float16).reshape(BLOCK, -1)


def unpacked(rows):
    rows = groups(rows).astype(jnp.float32)
    return (rows[: ROWS // 8] * jnp.exp2(rows[-1:])).reshape(ROWS, -1)


def after(value, *others):
    return lax.optimization_barrier((value, *others))[0]


def on_device(image_embeds, text_embeds, log_scale, bias):
    image_half, text_half = halves(image_embeds, text_embeds)
    scale_value = jnp.exp(log_scale[0])
    scalars = jnp.stack([scale_value * LOG2E, bias[0] * LOG2E, scale_value])
    above = send(image_half, before_up)
    below = send(image_half, before_down)
    texts = [text_half] + [send(text_half, move) for move in TEXT_MOVES]
    beside = send(image_half, other_core)
    opposite = send(after(image_half, above), y_far)
    first = [image_half, above, below]
    first_other = [beside, send(above, other_core), send(below, other_core)]

    mine, other, text_acc, sums = pairs(scalars, texts, first, first_other)
    second_other = send(after(opposite, sums), other_core)
    from_core = send(after(other, second_other), other_core)
    second, other, back0, back1, back2, back3 = pairs(
        scalars, texts, [opposite], [second_other], [text_acc, sums]
    )
    second_from_core = send(other, other_core)

    blocks = [slice(place * BLOCK, (place + 1) * BLOCK) for place in range(3)]
    above = packed(mine[blocks[1]], from_core[blocks[1]])
    below = packed(mine[blocks[2]], from_core[blocks[2]])
    totals, above, below, second_from_core = lax.optimization_barrier(
        (second[ROWS : ROWS + 8, :128], above, below, second_from_core)
    )
    opposite = packed(second, second_from_core)
    above = send(above, before_up, back=True)
    below = send(below, before_down, back=True)
    for move in NEAR_MOVES:
        totals = totals + send(totals, move)
    back1, back2, back3, opposite = after((back1, back2, back3, opposite), totals)
    up = send(back1.astype(jnp.float16), x_up, back=True)
    down = send(back2.astype(jnp.float16), x_down, back=True)
    far = send(after(back3, up, down).astype(jnp.float16), x_far, back=True)
    opposite = send(opposite, y_far, back=True)
    totals = after(totals, above, below, opposite)
    for move in FAR_MOVES:
        totals = totals + send(totals, move)
    totals = totals[:3, 0] / (ROWS * lax.axis_size("blk") * lax.axis_size("group"))

    text_sum = back0
    for rows in (up, down, far):
        text_sum = text_sum + unpacked(rows)
    image_sum = mine[:ROWS] + from_core[:ROWS]
    for rows in (opposite, above, below):
        image_sum = image_sum + unpacked(rows)
    grad_text = tangent_part(scalars, text_embeds, text_sum)
    grad_image = tangent_part(scalars, image_embeds, image_sum)
    return (totals[0:1], grad_image, grad_text, scale_value * totals[2:3], totals[1:2])


def solution(mesh):
    return jax.shard_map(
        on_device,
        mesh=mesh,
        in_specs=(P(AXES, None), P(AXES, None), P(), P()),
        out_specs=(P(), P(AXES, None), P(AXES, None), P(), P()),
        check_vma=False,
    )
```

```python
import functools

import jax
import jax.numpy as jnp
from jax import lax
from jax.experimental import pallas as pl
from jax.experimental.pallas import tpu as pltpu
from jax.sharding import PartitionSpec as P

AXES = ("blk", "group")
EPS = 1e-06
LOG2E = 1.4426950408889634
LN2 = 0.6931471805599453
ROWS = 256
BLOCK = 272
CHUNK = 16
LANES = 128
VMEM_LIMIT = 32 * 1024 * 1024


def place_index(z, y, x, core):
    z, y, x, core = z % 4, y % 4, x % 4, core % 2
    return (z * 2 + y % 2) * 16 + (y // 2) * 8 + x * 2 + core


def places():
    return [(z, y, x, c) for z in range(4) for y in range(4) for x in range(4) for c in range(2)]


def send(value, moved, back=False):
    pairs = [(place_index(*place), place_index(*moved(*place))) for place in places()]
    if back:
        pairs = [(target, source) for source, target in pairs]
    return lax.ppermute(value, AXES, pairs)


def other_core(z, y, x, c):
    return z, y, x, 1 - c


def x_up(z, y, x, c):
    return z, y, x + 1, c


def x_down(z, y, x, c):
    return z, y, x - 1, c


def x_far(z, y, x, c):
    return z, y, x + 2, c


def y_far(z, y, x, c):
    return z, y + 2, x, c


def before_up(z, y, x, c):
    return (z, y + 1, x, c) if y % 2 else (z - 1, y + 1, x, c)


def before_down(z, y, x, c):
    return (z, y - 1, x, c) if y % 2 else (z - 1, y - 1, x, c)


TEXT_MOVES = (x_up, x_down, x_far)
IMAGE_MOVES = (y_far, before_up, before_down)
NEAR_MOVES = (
    lambda z, y, x, c: (z, y, x ^ 1, c),
    lambda z, y, x, c: (z, y, x ^ 2, c),
    other_core,
)
FAR_MOVES = (
    lambda z, y, x, c: (z ^ 1, y, x, c),
    lambda z, y, x, c: (z ^ 2, y, x, c),
    lambda z, y, x, c: (z, y ^ 1, x, c),
    lambda z, y, x, c: (z, y ^ 2, x, c),
)


PARTS = 4


def part_copies(sources, targets, sems):
    rows = ROWS // PARTS
    return [
        [
            pltpu.make_async_copy(
                source.at[pl.ds(part * rows, rows)], target.at[pl.ds(part * rows, rows)], sems.at[part, place]
            )
            for place, (source, target) in enumerate(zip(sources, targets))
        ]
        for part in range(PARTS)
    ]


def by_parts(work, sources, held, results, targets, in_sems, out_sems):
    inward = part_copies(sources, held, in_sems)
    outward = part_copies(results, targets, out_sems)
    for copies in inward:
        for copy in copies:
            copy.start()
    for part in range(PARTS):
        for copy in inward[part]:
            copy.wait()
        work(slice(part * (ROWS // PARTS), (part + 1) * (ROWS // PARTS)))
        for copy in outward[part]:
            copy.start()
    for copies in outward:
        for copy in copies:
            copy.wait()


def halves_kernel(image_ref, text_ref, image_half_ref, text_half_ref, *buffers):
    held, results, sems = buffers[:2], buffers[2:4], buffers[4:]

    def work(part):
        for ref, half_ref in zip(held, results):
            rows = ref[part, :]
            length = jnp.sqrt(jnp.sum(rows * rows, axis=1, keepdims=True) + EPS)
            half_ref[part, :] = (rows * (1.0 / length)).astype(jnp.bfloat16)

    by_parts(work, (image_ref, text_ref), held, results, (image_half_ref, text_half_ref), *sems)


def halves(image_embeds, text_embeds):
    shape = image_embeds.shape
    half = jax.ShapeDtypeStruct(shape, jnp.bfloat16)
    anywhere = pl.BlockSpec(memory_space=pl.ANY)
    return pl.pallas_call(
        halves_kernel,
        in_specs=[anywhere] * 2,
        out_specs=[anywhere] * 2,
        out_shape=(half, half),
        scratch_shapes=[pltpu.VMEM(shape, jnp.float32)] * 2
        + [pltpu.VMEM(shape, jnp.bfloat16)] * 2
        + [pltpu.SemaphoreType.DMA((PARTS, 2))] * 2,
        name="halves",
    )(image_embeds, text_embeds)


def log1p(value):
    small = value * (1.0 - value * (0.5 - value * (1.0 / 3.0)))
    return jnp.where(value < 1e-3, small, jnp.log(1.0 + value))


def pair_terms(dots_ref, weights_ref, scale, shift, sums_ref, first_step):
    rows, cols = dots_ref.shape
    offset = jnp.where(first_step, 0, -2 * rows)
    for first_col in range(0, cols, LANES):
        relu = weight_sum = dot_sum = product = jnp.zeros((8, LANES), jnp.float32)
        for first_row in range(0, rows, CHUNK):
            place = (slice(first_row, first_row + CHUNK), slice(first_col, first_col + LANES))
            dots = dots_ref[place]
            logits = dots * scale + shift
            decay = jnp.exp2(jnp.minimum(logits, -logits))
            above = 1.0 + decay
            share = pl.reciprocal(above, approx=True)
            share = share * (2.0 - above * share)
            marked = first_row < ROWS and first_col <= first_row < first_col + LANES
            if marked:
                row = lax.broadcasted_iota(jnp.int32, (CHUNK, LANES), 0) + first_row
                col = lax.broadcasted_iota(jnp.int32, (CHUNK, LANES), 1) + first_col
                same = row - col == offset
                logits = jnp.where(same, -logits, logits)
            weights = jnp.where(logits >= 0, share, decay * share)
            if marked:
                weights = jnp.where(same, -weights, weights)
            weights_ref[place] = weights.astype(jnp.bfloat16)
            positive = jnp.maximum(logits, 0.0)
            weighted = weights * dots
            for first in range(0, CHUNK, 8):
                part = slice(first, first + 8)
                relu = relu + positive[part]
                weight_sum = weight_sum + weights[part]
                dot_sum = dot_sum + weighted[part]
                product = product * above[part] + decay[part]
        sums_ref[0] += relu * LN2 + log1p(product)
        sums_ref[1] += weight_sum
        sums_ref[2] += dot_sum


def largest(value):
    return fold_max(jnp.max(jnp.abs(value).reshape(value.shape[0] // 8, 8, value.shape[1]), axis=0))


def fold_max(value):
    total = value[:, 0:128]
    for first in range(128, value.shape[1], 128):
        total = jnp.maximum(total, value[:, first : first + 128])
    return total


def power_of(limit):
    return jnp.floor(jnp.log2(jnp.maximum(limit, 1e-30))) + 1.0


def pairs_kernel(count, earlier, last, *refs):
    refs = list(refs)
    take = lambda number: [refs.pop(0) for _ in range(number)]
    (scalars_ref,) = take(1)
    text_refs, mine_refs, other_refs = take(4), take(count), take(count)
    prior_text_ref, prior_sums_ref = take(2) if earlier else (None, None)
    mine_acc_ref, other_acc_ref = take(2)
    back_refs = take(4) if last else None
    text_acc_ref, sums_ref = take(2)
    text_ref, images_ref, dots_ref, weights_ref, limit_ref = refs
    step = pl.program_id(0)
    scale, shift = scalars_ref[0], scalars_ref[1]
    width = text_ref.shape[1]

    @pl.when(step == 0)
    def _():
        sums_ref[...] = prior_sums_ref[...] if earlier else jnp.zeros_like(sums_ref)
        limit_ref[...] = jnp.zeros_like(limit_ref)
        for place, ref in enumerate(text_refs):
            text_ref[place * ROWS : (place + 1) * ROWS, :] = ref[...]

    for place in range(count):

        @pl.when(step == place)
        def _():
            images_ref[:ROWS, :] = mine_refs[place][...]
            images_ref[ROWS:, :] = other_refs[place][...]

    dots_ref[...] = lax.dot_general(
        images_ref[...], text_ref[...], (((1,), (1,)), ((), ())), preferred_element_type=jnp.float32
    )
    pair_terms(dots_ref, weights_ref, scale, shift, sums_ref, step == 0 if not earlier else step < 0)
    acc = jnp.dot(weights_ref[...], text_ref[...], preferred_element_type=jnp.float32)
    limit_ref[...] = jnp.maximum(limit_ref[...], largest(acc))
    mine_acc_ref[:ROWS, :] = acc[:ROWS]
    other_acc_ref[:ROWS, :] = acc[ROWS:]
    power = power_of(jnp.full((8, width), jnp.max(limit_ref[...])))
    sums = power
    if last:
        row = lax.broadcasted_iota(jnp.int32, (8, width), 0)
        for place in range(3):
            sums = jnp.where(row == place, jnp.sum(sums_ref[place]), sums)
    for ref in (mine_acc_ref, other_acc_ref):
        ref[ROWS : ROWS + 8, :] = sums
        ref[ROWS + 8 :, :] = power
    back = lax.dot_general(
        weights_ref[...], images_ref[...], (((0,), (0,)), ((), ())), preferred_element_type=jnp.float32
    )
    if earlier:
        text_acc_ref[...] = prior_text_ref[...] + back
    else:

        @pl.when(step == 0)
        def _():
            text_acc_ref[...] = back

        @pl.when(step != 0)
        def _():
            text_acc_ref[...] += back

    if last:
        back_refs[0][...] = text_acc_ref[:ROWS, :]
        power = power_of(jnp.full((8, width), jnp.max(largest(text_acc_ref[ROWS:, :])))) - 10.0
        factor = jnp.exp2(-power)[:1]
        for place, ref in enumerate(back_refs[1:]):
            ref[:ROWS, :] = text_acc_ref[(place + 1) * ROWS : (place + 2) * ROWS, :] * factor
            ref[ROWS:, :] = jnp.concatenate([power, power], axis=0)


def pairs(scalars, texts, mine, other, prior=None):
    width = mine[0].shape[1]
    count = len(mine)
    last = prior is not None
    rows = 4 * ROWS
    unit = pl.BlockSpec((ROWS, width), lambda k: (0, 0))
    block = pl.BlockSpec((BLOCK, width), lambda k: (0, 0))
    each = pl.BlockSpec((BLOCK, width), lambda k: (k, 0))
    whole = pl.BlockSpec((rows, width), lambda k: (0, 0))
    sums = pl.BlockSpec((3, 8, 128), lambda k: (0, 0, 0))

    def shape(*dims):
        return jax.ShapeDtypeStruct(dims, jnp.float32)

    in_specs = [pl.BlockSpec(memory_space=pltpu.SMEM)] + [unit] * (4 + 2 * count)
    operands = [scalars, *texts, *mine, *other]
    out_specs = [each, each]
    out_shape = [shape(count * BLOCK, width)] * 2
    scratch = []
    if last:
        in_specs += [whole, sums]
        operands += prior
        out_specs += [unit, block, block, block]
        out_shape += [shape(ROWS, width)] + [shape(BLOCK, width)] * 3
        scratch += [pltpu.VMEM((rows, width), jnp.float32), pltpu.VMEM((3, 8, 128), jnp.float32)]
    else:
        out_specs += [whole, sums]
        out_shape += [shape(rows, width), shape(3, 8, 128)]
    return pl.pallas_call(
        functools.partial(pairs_kernel, count, last, last),
        grid=(count,),
        in_specs=in_specs,
        out_specs=out_specs,
        out_shape=out_shape,
        scratch_shapes=scratch
        + [
            pltpu.VMEM((rows, width), jnp.bfloat16),
            pltpu.VMEM((2 * ROWS, width), jnp.bfloat16),
            pltpu.VMEM((2 * ROWS, rows), jnp.float32),
            pltpu.VMEM((2 * ROWS, rows), jnp.bfloat16),
            pltpu.VMEM((8, 128), jnp.float32),
        ],
        compiler_params=pltpu.CompilerParams(vmem_limit_bytes=VMEM_LIMIT),
        cost_estimate=pl.CostEstimate(
            flops=(20 if last else 6) * rows * 2 * count * ROWS * width, bytes_accessed=1 << 20, transcendentals=3 * rows * 2 * count * ROWS
        ),
        name="pairs",
    )(*operands)


def tangent_kernel(scalars_ref, embeds_ref, accum_ref, out_ref):
    embeds = embeds_ref[...]
    accum = accum_ref[...]
    length = jnp.sqrt(jnp.sum(embeds * embeds, axis=1, keepdims=True) + EPS)
    inverse = 1.0 / length
    unit = embeds * inverse
    along = jnp.sum(unit * accum, axis=1, keepdims=True)
    out_ref[...] = (accum - unit * along) * (scalars_ref[2] * inverse)


def tangent_part(scalars, embeds, accum):
    return pl.pallas_call(
        tangent_kernel,
        in_specs=[pl.BlockSpec(memory_space=pltpu.SMEM)] + [pl.BlockSpec(memory_space=pltpu.VMEM)] * 2,
        out_shape=jax.ShapeDtypeStruct(embeds.shape, jnp.float32),
        name="tangent",
    )(scalars, embeds, accum)


def groups(rows):
    return rows.reshape(rows.shape[0] // 8, 8, rows.shape[1])


def packed(mine, other):
    mine, other = groups(mine), groups(other)
    power = jnp.maximum(mine[-1:], other[-1:]) - 9.0
    group = lax.broadcasted_iota(jnp.int32, mine.shape, 0)
    rows = jnp.where(group < ROWS // 8, (mine + other) * jnp.exp2(-power), power)
    return rows.astype(jnp.float16).reshape(BLOCK, -1)


def unpacked(rows):
    rows = groups(rows).astype(jnp.float32)
    return (rows[: ROWS // 8] * jnp.exp2(rows[-1:])).reshape(ROWS, -1)


def after(value, *others):
    return lax.optimization_barrier((value, *others))[0]


def on_device(image_embeds, text_embeds, log_scale, bias):
    image_half, text_half = halves(image_embeds, text_embeds)
    scale_value = jnp.exp(log_scale[0])
    scalars = jnp.stack([scale_value * LOG2E, bias[0] * LOG2E, scale_value])
    above = send(image_half, before_up)
    below = send(image_half, before_down)
    texts = [text_half] + [send(text_half, move) for move in TEXT_MOVES]
    beside = send(image_half, other_core)
    opposite = send(after(image_half, above), y_far)
    first = [image_half, above, below]
    first_other = [beside, send(above, other_core), send(below, other_core)]

    mine, other, text_acc, sums = pairs(scalars, texts, first, first_other)
    second_other = send(after(opposite, sums), other_core)
    from_core = send(after(other, second_other), other_core)
    second, other, back0, back1, back2, back3 = pairs(
        scalars, texts, [opposite], [second_other], [text_acc, sums]
    )
    second_from_core = send(other, other_core)

    blocks = [slice(place * BLOCK, (place + 1) * BLOCK) for place in range(3)]
    above = packed(mine[blocks[1]], from_core[blocks[1]])
    below = packed(mine[blocks[2]], from_core[blocks[2]])
    totals, above, below, second_from_core = lax.optimization_barrier(
        (second[ROWS : ROWS + 8, :128], above, below, second_from_core)
    )
    opposite = packed(second, second_from_core)
    above = send(above, before_up, back=True)
    below = send(below, before_down, back=True)
    for move in NEAR_MOVES:
        totals = totals + send(totals, move)
    back1, back2, back3, opposite = after((back1, back2, back3, opposite), totals)
    up = send(back1.astype(jnp.float16), x_up, back=True)
    down = send(back2.astype(jnp.float16), x_down, back=True)
    far = send(after(back3, up, down).astype(jnp.float16), x_far, back=True)
    opposite = send(opposite, y_far, back=True)
    totals = after(totals, above, below, opposite)
    for move in FAR_MOVES:
        totals = totals + send(totals, move)
    totals = totals[:3, 0] / (ROWS * lax.axis_size("blk") * lax.axis_size("group"))

    text_sum = back0
    for rows in (up, down, far):
        text_sum = text_sum + unpacked(rows)
    image_sum = mine[:ROWS] + from_core[:ROWS]
    for rows in (opposite, above, below):
        image_sum = image_sum + unpacked(rows)
    grad_text = tangent_part(scalars, text_embeds, text_sum)
    grad_image = tangent_part(scalars, image_embeds, image_sum)
    return (totals[0:1], grad_image, grad_text, scale_value * totals[2:3], totals[1:2])


def solution(mesh):
    return jax.shard_map(
        on_device,
        mesh=mesh,
        in_specs=(P(AXES, None), P(AXES, None), P(), P()),
        out_specs=(P(), P(AXES, None), P(AXES, None), P(), P()),
        check_vma=False,
    )
```
